32 devices in a mesh: fsdp: 4 (over x, core), ctx: 8 (over z, y).
Axes of the slice: x: 2, y: 2, z: 4, core: 2. Of those that a mesh axis runs over, the one named last changes fastest.
Arguments:
- query_branch: bfloat16 [4, 2048, 4096], P('fsdp', 'ctx'), may hold values from -6 to 6
- key_branch: bfloat16 [4, 2048, 4096], P('fsdp', 'ctx'), may hold values from -6 to 6
- value_branch: bfloat16 [4, 2048, 4096], P('fsdp', 'ctx'), may hold values from -6 to 6
- cotangent: bfloat16 [4, 2048, 4096], P('fsdp', 'ctx'), may hold values from -6 to 6
- quantized_weight_codes: int32 [4096, 4096], P('ctx', 'fsdp'), may hold values from 0 to 15
- scale_code_bytes: int32 [4096, 64], P('ctx', 'fsdp'), may hold values from 0 to 255
- row_scale_second: float32 [4096], P('ctx'), may hold values from 0.01 to 0.1
- filters: bfloat16 [256, 128], replicated, may hold values from -0.5 to 0.5
- channel_skip_weight: float32 [4096], replicated, may hold values from -6 to 6
- adapter_down_weight: bfloat16 [4096, 64], P('ctx'), may hold values from -0.09375 to 0.09375
- adapter_up_weight: bfloat16 [64, 4096], P(None, 'fsdp'), may hold values from -0.75 to 0.75
Outputs:
- output: bfloat16 [4, 2048, 4096], P('fsdp', 'ctx')
- grad_query: bfloat16 [4, 2048, 4096], P('fsdp', 'ctx')
- grad_key: bfloat16 [4, 2048, 4096], P('fsdp', 'ctx')
- grad_value: bfloat16 [4, 2048, 4096], P('fsdp', 'ctx')
- grad_down: bfloat16 [4096, 64], P('ctx')
- grad_up: bfloat16 [64, 4096], P(None, 'fsdp')
The draws below stay inside these ranges and needn't reach their ends.
All inputs are finite; a program needn't handle non-finite values.
Results may differ from the reference program's by a relative error of at most 0.0067.
Values may be sent and summed in bfloat16 or wider, within the bound.
A program may use at most 256 MiB of HBM per device.

```python
import math
import jax
import jax.numpy as jnp

OPERATOR_WIDTH = 4096
OUTPUT_FEATURES = 4096
FL = 128
ADAPTER_RANK = 64
QBLOCK = 64
SEQS = 4
SEQLEN = 2048
GROUPS = 256
SCALE_COLS = 64


def touch_ends(drawn, rng, least, top_value):
    longest = drawn.shape.index(max(drawn.shape))
    spots = []
    for shift in (0, 1):
        where = [jax.random.randint(jax.random.fold_in(rng, axis), (), 0, length) for axis, length in enumerate(drawn.shape)]
        where[longest] = (where[longest] + shift) % drawn.shape[longest]
        spots.append(tuple(where))
    return drawn.at[spots[0]].set(least).at[spots[1]].set(top_value)


def raised(entries, key, source, target, blocks, factor):
    owner, partner = [(jnp.arange(entries.shape[position]) // (entries.shape[position] // blocks)).reshape([-1 if axis == position else 1 for axis in range(entries.ndim)]) for position in (source, target)]
    chosen = jax.random.permutation(key, blocks)[partner]
    strong = (owner == chosen) | (owner == (partner + blocks // 2) % blocks)
    return jnp.where(strong, factor * entries, entries)


def block_levels(key, extent, split, low, largest):
    loudness = 1.0
    for axis_at, shards_of in split:
        steps = jax.random.uniform(jax.random.fold_in(jax.random.fold_in(key, 6), axis_at), (shards_of,), jnp.float32, low / len(split), largest / len(split))
        loudness = loudness * jnp.repeat(jnp.exp(steps), extent[axis_at] // shards_of).reshape((-1,) + (1,) * (len(extent) - 1 - axis_at))
    return loudness


def normal_values(rng, shape, spread, limit, cuts=(), kind=jnp.bfloat16):
    level = block_levels(rng, shape, cuts, -0.22, 0.18) if cuts else 1.0
    drawn = jax.random.normal(rng, shape, jnp.float32) * spread * level
    return jnp.minimum(jnp.maximum(drawn, -limit), limit).astype(kind)


def heavy_noise(rng, dims, width, most, pieces, heavy, held_as=jnp.bfloat16):
    values = width * jax.random.normal(rng, dims, jnp.float32)
    if pieces:
        values = values * block_levels(rng, dims, pieces, -0.22, 0.18)
    return jnp.clip(raised(values, jax.random.fold_in(rng, 3), *heavy), -most, most).astype(held_as)


def setup_inputs(seed: int = 0) -> dict:
    key_of = jax.random.split(jax.random.key(seed), 12)
    return {
        "query_branch": heavy_noise(key_of[0], (SEQS, SEQLEN, OPERATOR_WIDTH), 1.0, 6.0, ((0, 4), (1, 8)), (1, 2, 8, 2.0)),
        "key_branch": normal_values(key_of[1], (SEQS, SEQLEN, OPERATOR_WIDTH), 1.0, 6.0, ((0, 4), (1, 8))),
        "value_branch": normal_values(key_of[2], (SEQS, SEQLEN, OPERATOR_WIDTH), 1.0, 6.0, ((0, 4), (1, 8))),
        "cotangent": normal_values(key_of[3], (SEQS, SEQLEN, OUTPUT_FEATURES), 1.0, 6.0, ((0, 4), (1, 8))),
        "quantized_weight_codes": touch_ends(jax.random.randint(key_of[4], (OPERATOR_WIDTH, OUTPUT_FEATURES), 0, 16), jax.random.fold_in(key_of[4], 1), 0, 15).astype(jnp.int32),
        "scale_code_bytes": touch_ends(jax.random.randint(key_of[5], (OPERATOR_WIDTH, SCALE_COLS), 0, 256), jax.random.fold_in(key_of[5], 1), 0, 255).astype(jnp.int32),
        "row_scale_second": jnp.clip(jnp.exp(math.log(0.1) - 2.3025851 * jax.random.uniform(key_of[6], (OPERATOR_WIDTH,), jnp.float32) ** block_levels(key_of[6], (OPERATOR_WIDTH,), ((0, 8),), -0.2, 0.2)), 0.01, 0.1),
        "filters": normal_values(key_of[7], (GROUPS, FL), FL ** -0.5, 0.5),
        "channel_skip_weight": normal_values(key_of[8], (OPERATOR_WIDTH,), 1.0, 6.0, (), jnp.float32),
        "adapter_down_weight": normal_values(key_of[9], (OPERATOR_WIDTH, ADAPTER_RANK), OPERATOR_WIDTH ** -0.5, 0.09375, ((0, 8),)),
        "adapter_up_weight": normal_values(key_of[10], (ADAPTER_RANK, OUTPUT_FEATURES), ADAPTER_RANK ** -0.5, 0.75, ((1, 4),)),
    }


normal_levels = (-1.0, -0.6961928009986877, -0.5250730514526367, -0.39491748809814453, -0.28444138169288635, -0.18477343022823334, -0.09105003625154495, 0.0, 0.07958029955625534, 0.16093020141124725, 0.24611230194568634, 0.33791524171829224, 0.44070982933044434, 0.5626170039176941, 0.7229568362236023, 1.0)
adapter_scale = 0.25

def dequantize(quantized_weight_codes, scale_code_bytes, row_scale_second):
    level_table = jnp.array(normal_levels, jnp.float32)
    levels = level_table[quantized_weight_codes]
    absmax = row_scale_second[:, None] * (scale_code_bytes.astype(jnp.float32) + 1.0) / 256.0
    absmax = jnp.repeat(absmax, QBLOCK, axis=1)
    return (levels * absmax).astype(jnp.bfloat16)

def toeplitz(filter_taps, filter_len):
    groups = filter_taps.shape[0]
    padded = jnp.concatenate([filter_taps, jnp.zeros((groups, filter_len), filter_taps.dtype)], 1)
    repeated = jnp.tile(padded, (1, filter_len))[:, :filter_len * (2 * filter_len - 1)]
    return repeated.reshape(groups, filter_len, 2 * filter_len - 1)

def block_conv(extended, toep, filter_len):
    row_count = extended.shape[0] - (filter_len - 1)
    blocks = row_count // filter_len
    current = extended[:row_count].reshape(blocks, filter_len, -1)
    following = jnp.concatenate([extended[filter_len:], jnp.zeros((1, extended.shape[1]), extended.dtype)], 0)
    following = following.reshape(blocks, filter_len, -1)[:, :filter_len - 1]
    windows = jnp.concatenate([current, following], 1)
    windows = windows.reshape(blocks, 2 * filter_len - 1, toep.shape[0], -1)
    result = jnp.einsum('gts,bsgk->btgk', toep.astype(jnp.float32), windows.astype(jnp.float32))
    return result.reshape(row_count, -1)

def reference(query_branch, key_branch, value_branch, cotangent, quantized_weight_codes, scale_code_bytes, row_scale_second, filters, channel_skip_weight, adapter_down_weight, adapter_up_weight):
    filter_len = filters.shape[1]
    channels = query_branch.shape[2]
    weight_matrix = dequantize(quantized_weight_codes, scale_code_bytes, row_scale_second)
    ahead_toep = toeplitz(jnp.flip(filters, 1), filter_len)
    back_toep = toeplitz(filters, filter_len)
    multiplier = adapter_scale / math.sqrt(query_branch.shape[0] * query_branch.shape[1])
    outputs, grad_queries, grad_keys, grad_values = ([], [], [], [])
    down_accumulator = jnp.zeros(adapter_down_weight.shape, jnp.float32)
    up_accumulator = jnp.zeros(adapter_up_weight.shape, jnp.float32)
    for sequence in range(query_branch.shape[0]):
        query_float = query_branch[sequence].astype(jnp.float32)
        key_float = key_branch[sequence].astype(jnp.float32)
        value_float = value_branch[sequence].astype(jnp.float32)
        output_gradient = cotangent[sequence]
        mixed = (key_float * value_float).astype(jnp.bfloat16)
        extended = jnp.concatenate([jnp.zeros((filter_len - 1, channels), mixed.dtype), mixed], 0)
        gated = block_conv(extended, ahead_toep, filter_len) + channel_skip_weight * mixed.astype(jnp.float32)
        gated_signal = (query_float * gated).astype(jnp.bfloat16)
        down_projection = jnp.dot(gated_signal, adapter_down_weight, preferred_element_type=jnp.float32).astype(jnp.bfloat16)
        output = jnp.dot(gated_signal, weight_matrix, preferred_element_type=jnp.float32) + adapter_scale * jnp.dot(down_projection, adapter_up_weight, preferred_element_type=jnp.float32)
        outputs.append(output.astype(jnp.bfloat16))
        backward_up_term = jnp.dot(output_gradient, adapter_up_weight.T, preferred_element_type=jnp.float32).astype(jnp.bfloat16)
        backward_gradient = jnp.dot(output_gradient, weight_matrix.T, preferred_element_type=jnp.float32) + adapter_scale * jnp.dot(backward_up_term, adapter_down_weight.T, preferred_element_type=jnp.float32)
        grad_queries.append((backward_gradient * gated).astype(jnp.bfloat16))
        grad_gated = (backward_gradient * query_float).astype(jnp.bfloat16)
        extended_back = jnp.concatenate([grad_gated, jnp.zeros((filter_len - 1, channels), grad_gated.dtype)], 0)
        grad_mixed = block_conv(extended_back, back_toep, filter_len) + channel_skip_weight * grad_gated.astype(jnp.float32)
        grad_keys.append((grad_mixed * value_float).astype(jnp.bfloat16))
        grad_values.append((grad_mixed * key_float).astype(jnp.bfloat16))
        down_accumulator = down_accumulator + jnp.dot(gated_signal.T, backward_up_term, preferred_element_type=jnp.float32)
        up_accumulator = up_accumulator + jnp.dot(down_projection.T, output_gradient, preferred_element_type=jnp.float32)
    return (jnp.stack(outputs), jnp.stack(grad_queries), jnp.stack(grad_keys), jnp.stack(grad_values), (multiplier * down_accumulator).astype(jnp.bfloat16), (multiplier * up_accumulator).astype(jnp.bfloat16))
```

```python
import functools
import math

import jax
import jax.numpy as jnp
from jax import lax
from jax.experimental import pallas as pl
from jax.experimental.pallas import tpu as pltpu
from jax.sharding import PartitionSpec as P

QBLOCK = 64
LANES = 128
MESH = pl.DeviceIdType.MESH
VMEM_LIMIT = 56 * 1024 * 1024

normal_levels = (
    -1.0,
    -0.6961928009986877,
    -0.5250730514526367,
    -0.39491748809814453,
    -0.28444138169288635,
    -0.18477343022823334,
    -0.09105003625154495,
    0.0,
    0.07958029955625534,
    0.16093020141124725,
    0.24611230194568634,
    0.33791524171829224,
    0.44070982933044434,
    0.5626170039176941,
    0.7229568362236023,
    1.0,
)
adapter_scale = 0.25


def from_behind(shard, axis, by):
    count = lax.axis_size(axis)
    pairs = [(i, i + by) for i in range(count) if 0 <= i + by < count]
    return lax.ppermute(shard, axis, pairs)


def dequantize(quantized_weight_codes, scale_code_bytes, row_scale_second):
    levels = jnp.zeros(quantized_weight_codes.shape, jnp.float32)
    for number in range(16):
        levels = jnp.where(quantized_weight_codes == number, normal_levels[number], levels)
    absmax = row_scale_second[:, None] * (scale_code_bytes.astype(jnp.float32) + 1.0) / 256.0
    absmax = jnp.repeat(absmax, QBLOCK, axis=1)
    return (levels * absmax).astype(jnp.bfloat16)


def gather_kernel(line, own_ref, all_ref, local_sem, recv, sib_recv, z_send, y_send, x_send, sib_send):
    f, c = lax.axis_index("fsdp"), lax.axis_index("ctx")
    x, k, z, y = f // 2, f % 2, c // 2, c % 2
    half = own_ref.shape[0] // 2
    x_peer = (lax.rem(f + 2, 4), c)
    sibling = (f + 1 - 2 * k, c)
    y_peer = (f, c + 1 - 2 * y)
    z_up, z_down = (f, c + 2), (f, c - 2)

    def place(h, xx, yy, zz, kk):
        rows = pl.ds((2 * zz + yy) * (2 * half) + h * half, half)
        return all_ref.at[2 * xx + kk, rows, :]

    def copy(h, xx, yy, zz, send, arrive, to):
        block = place(h, xx, yy, zz, k)
        return pltpu.make_async_remote_copy(
            src_ref=block, dst_ref=block, send_sem=send, recv_sem=arrive,
            device_id=to, device_id_type=MESH,
        )

    def along_x(h, xx, yy, zz):
        return copy(h, xx, yy, zz, x_send.at[h, xx, yy, zz], recv.at[h, xx, yy, zz], x_peer)

    def along_y(h, xx, yy, zz):
        return copy(h, xx, yy, zz, y_send.at[h, xx, yy, zz], recv.at[h, xx, yy, zz], y_peer)

    def along_z(h, zz, up):
        return copy(
            h, x, y, zz, z_send.at[h, up, zz], recv.at[h, x, y, zz], z_up if up else z_down
        )

    def to_sibling(h, xx, yy, zz):
        return copy(h, xx, yy, zz, sib_send.at[h, xx, yy, zz], sib_recv.at[h, xx, yy, zz], sibling)

    def arrived(h, xx, yy, zz):
        along_x(h, xx, yy, zz).wait_recv()

    def places(step):
        yield z - step, z - step >= 0, True
        if step:
            yield z + step, z + step < line, False

    def first(step):
        for zz, there, upward in places(step):
            @pl.when(there)
            def _():
                for h in (0, 1):
                    if step:
                        arrived(h, x, y, zz)
                    if upward:
                        @pl.when(z + 1 < line)
                        def _():
                            along_z(h, zz, 1).start()
                    if not upward or step == 0:
                        @pl.when(z > 0)
                        def _():
                            along_z(h, zz, 0).start()
                along_y(0, x, y, zz).start()
                along_x(1, x, y, zz).start()
                for h in (0, 1):
                    to_sibling(h, x, y, zz).start()

    def second(step):
        for zz, there, _ in places(step):
            @pl.when(there)
            def _():
                along_x(0, x, y, zz).start()
                along_y(1, x, y, zz).start()
                arrived(0, x, 1 - y, zz)
                along_x(0, x, 1 - y, zz).start()
                arrived(1, 1 - x, y, zz)
                along_y(1, 1 - x, y, zz).start()
                to_sibling(0, x, 1 - y, zz).start()
                to_sibling(1, 1 - x, y, zz).start()

    def third(step):
        for zz, there, _ in places(step):
            @pl.when(there)
            def _():
                for other in (y, 1 - y):
                    arrived(0, 1 - x, other, zz)
                    to_sibling(0, 1 - x, other, zz).start()
                for other in (x, 1 - x):
                    arrived(1, other, 1 - y, zz)
                    to_sibling(1, other, 1 - y, zz).start()

    mine = pltpu.make_async_copy(
        own_ref, all_ref.at[f, pl.ds(c * (2 * half), 2 * half), :], local_sem
    )
    mine.start()
    barrier = pltpu.get_barrier_semaphore()
    for peer in (x_peer, y_peer, sibling):
        pl.semaphore_signal(barrier, inc=1, device_id=peer, device_id_type=MESH)

    @pl.when(z + 1 < line)
    def _():
        pl.semaphore_signal(barrier, inc=1, device_id=z_up, device_id_type=MESH)

    @pl.when(z > 0)
    def _():
        pl.semaphore_signal(barrier, inc=1, device_id=z_down, device_id_type=MESH)

    inside = jnp.logical_and(z > 0, z + 1 < line)

    @pl.when(inside)
    def _():
        pl.semaphore_wait(barrier, 5)

    @pl.when(jnp.logical_not(inside))
    def _():
        pl.semaphore_wait(barrier, 4)

    mine.wait()
    for step in range(line + 2):
        if step < line:
            first(step)
        if 1 <= step <= line:
            second(step - 1)
        if step >= 2:
            third(step - 2)

    def finish(zz, carry):
        for xx in (0, 1):
            for yy in (0, 1):
                for h in (0, 1):
                    to_sibling(h, xx, yy, zz).wait()
        for yy in (0, 1):
            along_x(0, x, yy, zz).wait_send()
        along_x(1, x, y, zz).wait_send()
        for xx in (0, 1):
            along_y(1, xx, y, zz).wait_send()
        along_y(0, x, y, zz).wait_send()
        for h in (0, 1):
            @pl.when(jnp.logical_and(zz <= z, z + 1 < line))
            def _():
                along_z(h, zz, 1).wait_send()

            @pl.when(jnp.logical_and(zz >= z, z > 0))
            def _():
                along_z(h, zz, 0).wait_send()
        return carry

    lax.fori_loop(0, line, finish, 0)


def gather_weight(piece, n_f, n_c):
    rows, columns = piece.shape
    line = n_c // 2
    blocks = (2, 2, 2, line)
    return pl.pallas_call(
        functools.partial(gather_kernel, line),
        out_shape=jax.ShapeDtypeStruct((n_f, n_c * rows, columns), piece.dtype),
        in_specs=[pl.BlockSpec(memory_space=pl.ANY)],
        out_specs=pl.BlockSpec(memory_space=pl.ANY),
        scratch_shapes=[
            pltpu.SemaphoreType.DMA,
            pltpu.SemaphoreType.DMA(blocks),
            pltpu.SemaphoreType.DMA(blocks),
            pltpu.SemaphoreType.DMA((2, 2, line)),
            pltpu.SemaphoreType.DMA(blocks),
            pltpu.SemaphoreType.DMA(blocks),
            pltpu.SemaphoreType.DMA(blocks),
        ],
        compiler_params=pltpu.CompilerParams(
            collective_id=0, has_side_effects=True, vmem_limit_bytes=VMEM_LIMIT
        ),
        cost_estimate=pl.CostEstimate(
            flops=0, bytes_accessed=16 * n_f * n_c * rows * columns, transcendentals=0
        ),
        name="gather_weight",
    )(piece)


def conv_blocks(base, windows):
    filters_here, width = base.shape
    taps = width // 2
    toep = jnp.concatenate(
        [
            pltpu.roll(
                jnp.broadcast_to(base[g : g + 1], (taps, width)), 0, 1, stride=1, stride_axis=0
            )
            for g in range(filters_here)
        ],
        0,
    ).astype(jnp.bfloat16)
    product = jnp.dot(toep, jnp.concatenate(windows, 1), preferred_element_type=jnp.float32)
    lanes = lax.broadcasted_iota(jnp.int32, (taps, LANES), 1) // (LANES // filters_here)
    results = []
    for b in range(len(windows)):
        part = product[:, b * LANES : (b + 1) * LANES]
        chosen = part[:taps]
        for g in range(1, filters_here):
            chosen = jnp.where(lanes == g, part[g * taps : (g + 1) * taps], chosen)
        results.append(chosen)
    return jnp.concatenate(results, 0)


def ahead_kernel(query_ref, key_ref, value_ref, before_ref, base_ref, skip_ref, gated_ref, input_ref):
    taps = base_ref.shape[1] // 2
    mixed = (key_ref[...].astype(jnp.float32) * value_ref[...].astype(jnp.float32)).astype(
        jnp.bfloat16
    )
    joined = jnp.concatenate([before_ref[...], mixed], 0)
    windows = [joined[b * taps : (b + 2) * taps] for b in range(mixed.shape[0] // taps)]
    gated = conv_blocks(base_ref[...], windows) + skip_ref[...] * mixed.astype(jnp.float32)
    gated_ref[...] = gated
    input_ref[...] = (query_ref[...].astype(jnp.float32) * gated).astype(jnp.bfloat16)


def back_kernel(grad_ref, after_ref, key_ref, value_ref, base_ref, skip_ref, gk_ref, gv_ref):
    taps = base_ref.shape[1] // 2
    grad = grad_ref[...]
    joined = jnp.concatenate([grad, after_ref[...]], 0)
    windows = [joined[b * taps : (b + 2) * taps] for b in range(grad.shape[0] // taps)]
    grad_mixed = conv_blocks(base_ref[...], windows) + skip_ref[...] * grad.astype(jnp.float32)
    gk_ref[...] = (grad_mixed * value_ref[...].astype(jnp.float32)).astype(jnp.bfloat16)
    gv_ref[...] = (grad_mixed * key_ref[...].astype(jnp.float32)).astype(jnp.bfloat16)


def tile_call(kernel, operands, out_types, groups, name):
    rows, channels = operands[0].shape
    tiles = channels // LANES

    def spec(array):
        if array.shape[0] == groups:
            if array.shape[1] != channels:
                return pl.BlockSpec((groups // tiles, array.shape[1]), lambda i: (i, 0))
        return pl.BlockSpec((array.shape[0], LANES), lambda i: (0, i))

    return pl.pallas_call(
        kernel,
        grid=(tiles,),
        in_specs=[spec(a) for a in operands],
        out_specs=[pl.BlockSpec((rows, LANES), lambda i: (0, i)) for _ in out_types],
        out_shape=[jax.ShapeDtypeStruct((rows, channels), t) for t in out_types],
        compiler_params=pltpu.CompilerParams(vmem_limit_bytes=VMEM_LIMIT),
        cost_estimate=pl.CostEstimate(
            flops=rows * channels * 4096, bytes_accessed=rows * channels * 12, transcendentals=0
        ),
        name=name,
    )(*operands)


def product_kernel(
    weight_ref, cot_ref, input_ref, gated_ref, query_ref, back_up_ref, down_ref, proj_ref, up_ref,
    out_ref, gq_ref, gg_ref, total,
):
    step = pl.program_id(0)
    parts, _, width = weight_ref.shape

    @pl.when(step == 0)
    def _():
        total[...] = adapter_scale * jnp.dot(
            proj_ref[...], up_ref[...], preferred_element_type=jnp.float32
        )

    nt = (((1,), (1,)), ((), ()))
    back = adapter_scale * lax.dot_general(
        back_up_ref[...], down_ref[...], nt, preferred_element_type=jnp.float32
    )
    for f in range(parts):
        columns = slice(f * width, (f + 1) * width)
        weight = weight_ref[f]
        back = back + lax.dot_general(
            cot_ref[:, columns], weight, nt, preferred_element_type=jnp.float32
        )
        total[:, columns] += jnp.dot(input_ref[...], weight, preferred_element_type=jnp.float32)
    gq_ref[...] = (back * gated_ref[...]).astype(jnp.bfloat16)
    gg_ref[...] = (back * query_ref[...].astype(jnp.float32)).astype(jnp.bfloat16)

    @pl.when(step == pl.num_programs(0) - 1)
    def _():
        out_ref[...] = total[...].astype(jnp.bfloat16)


def products(weight, cot, gated_input, gated, query, back_up, down, proj, up):
    parts, channels, width = weight.shape
    rows = cot.shape[0]
    features = parts * width
    rank = down.shape[1]
    block = 512
    whole = lambda i: (0, 0)
    tile = pl.BlockSpec((rows, block), lambda i: (0, i))
    return pl.pallas_call(
        product_kernel,
        grid=(channels // block,),
        in_specs=[
            pl.BlockSpec((parts, block, width), lambda i: (0, i, 0)),
            pl.BlockSpec((rows, features), whole),
            tile,
            tile,
            tile,
            pl.BlockSpec((rows, rank), whole),
            pl.BlockSpec((block, rank), lambda i: (i, 0)),
            pl.BlockSpec((rows, rank), whole),
            pl.BlockSpec((rank, features), whole),
        ],
        out_specs=[pl.BlockSpec((rows, features), whole), tile, tile],
        out_shape=[
            jax.ShapeDtypeStruct((rows, features), jnp.bfloat16),
            jax.ShapeDtypeStruct((rows, channels), jnp.bfloat16),
            jax.ShapeDtypeStruct((rows, channels), jnp.bfloat16),
        ],
        scratch_shapes=[pltpu.VMEM((rows, features), jnp.float32)],
        compiler_params=pltpu.CompilerParams(vmem_limit_bytes=VMEM_LIMIT),
        cost_estimate=pl.CostEstimate(
            flops=4 * rows * channels * features,
            bytes_accessed=2 * channels * features,
            transcendentals=0,
        ),
        name="products",
    )(weight, cot, gated_input, gated, query, back_up, down, proj, up)


def local(
    query_branch,
    key_branch,
    value_branch,
    cotangent,
    quantized_weight_codes,
    scale_code_bytes,
    row_scale_second,
    filters,
    channel_skip_weight,
    adapter_down_weight,
    adapter_up_weight,
):
    groups, filter_len = filters.shape
    query, key, value, cot = query_branch[0], key_branch[0], value_branch[0], cotangent[0]
    row_count = query.shape[0]
    n_f, n_c = lax.axis_size("fsdp"), lax.axis_size("ctx")
    token_count = query_branch.shape[0] * row_count * n_c * n_f
    multiplier = adapter_scale / math.sqrt(token_count)
    skip = channel_skip_weight[None]

    tail = row_count - filter_len
    mixed_tail = (
        key[tail:].astype(jnp.float32) * value[tail:].astype(jnp.float32)
    ).astype(jnp.bfloat16)
    before = from_behind(mixed_tail, "ctx", 1)
    piece = dequantize(quantized_weight_codes, scale_code_bytes, row_scale_second)
    up = lax.all_gather(adapter_up_weight, "fsdp", axis=1, tiled=True)
    down = lax.all_gather(adapter_down_weight, "ctx", axis=0, tiled=True)
    taps = filters.astype(jnp.float32)
    zeros = jnp.zeros((groups, filter_len), jnp.float32)
    back_base = jnp.concatenate([taps, zeros], 1)
    ahead_base = jnp.concatenate([zeros[:, :1], jnp.flip(taps, 1), zeros[:, 1:]], 1)

    weight = gather_weight(piece, n_f, n_c)
    gated, gated_input = tile_call(
        ahead_kernel,
        (query, key, value, before, ahead_base, skip),
        (jnp.float32, jnp.bfloat16),
        groups,
        "conv_ahead",
    )
    back_up = lax.dot_general(
        cot, up, (((1,), (1,)), ((), ())), preferred_element_type=jnp.float32
    ).astype(jnp.bfloat16)
    proj = jnp.dot(gated_input, down, preferred_element_type=jnp.float32).astype(jnp.bfloat16)
    over_rows = (((0,), (0,)), ((), ()))
    term_down = lax.dot_general(
        gated_input, back_up, over_rows, preferred_element_type=jnp.float32
    )
    term_up = lax.dot_general(proj, cot, over_rows, preferred_element_type=jnp.float32)
    part_down = lax.psum_scatter(term_down, "ctx", scatter_dimension=0, tiled=True)
    part_up = lax.psum_scatter(term_up, "fsdp", scatter_dimension=1, tiled=True)
    grad_down = multiplier * lax.psum(part_down, "fsdp")
    grad_up = multiplier * lax.psum(part_up, "ctx")

    output, grad_query, grad_gated = products(
        weight, cot, gated_input, gated, query, back_up, down, proj, up
    )
    after = from_behind(grad_gated[:filter_len], "ctx", -1)
    grad_key, grad_value = tile_call(
        back_kernel,
        (grad_gated, after, key, value, back_base, skip),
        (jnp.bfloat16, jnp.bfloat16),
        groups,
        "conv_back",
    )
    return (
        output[None],
        grad_query[None],
        grad_key[None],
        grad_value[None],
        grad_down.astype(jnp.bfloat16),
        grad_up.astype(jnp.bfloat16),
    )


def solution(mesh):
    return jax.shard_map(
        local,
        mesh=mesh,
        in_specs=(
            P("fsdp", "ctx", None),
            P("fsdp", "ctx", None),
            P("fsdp", "ctx", None),
            P("fsdp", "ctx", None),
            P("ctx", "fsdp"),
            P("ctx", "fsdp"),
            P("ctx"),
            P(),
            P(),
            P("ctx", None),
            P(None, "fsdp"),
        ),
        out_specs=(
            P("fsdp", "ctx", None),
            P("fsdp", "ctx", None),
            P("fsdp", "ctx", None),
            P("fsdp", "ctx", None),
            P("ctx", None),
            P(None, "fsdp"),
        ),
        check_vma=False,
    )
```

```python
import functools
import math

import jax
import jax.numpy as jnp
from jax import lax
from jax.experimental import pallas as pl
from jax.experimental.pallas import tpu as pltpu
from jax.sharding import PartitionSpec as P

QBLOCK = 64
LANES = 128
MESH = pl.DeviceIdType.MESH
VMEM_LIMIT = 56 * 1024 * 1024

normal_levels = (
    -1.0,
    -0.6961928009986877,
    -0.5250730514526367,
    -0.39491748809814453,
    -0.28444138169288635,
    -0.18477343022823334,
    -0.09105003625154495,
    0.0,
    0.07958029955625534,
    0.16093020141124725,
    0.24611230194568634,
    0.33791524171829224,
    0.44070982933044434,
    0.5626170039176941,
    0.7229568362236023,
    1.0,
)
adapter_scale = 0.25


def from_behind(shard, axis, by):
    count = lax.axis_size(axis)
    pairs = [(i, i + by) for i in range(count) if 0 <= i + by < count]
    return lax.ppermute(shard, axis, pairs)


def dequantize(quantized_weight_codes, scale_code_bytes, row_scale_second):
    levels = jnp.zeros(quantized_weight_codes.shape, jnp.float32)
    for number in range(16):
        levels = jnp.where(quantized_weight_codes == number, normal_levels[number], levels)
    absmax = row_scale_second[:, None] * (scale_code_bytes.astype(jnp.float32) + 1.0) / 256.0
    absmax = jnp.repeat(absmax, QBLOCK, axis=1)
    return (levels * absmax).astype(jnp.bfloat16)


def gather_kernel(
    line, tail_ref, own_ref, down_ref, up_ref, cot_ref, query_ref, key_ref, value_ref, base_ref, skip_ref,
    all_ref, gated_ref, input_ref, term_down_ref, term_up_ref, proj_ref, back_up_ref, down_out, up_out,
    before, down_all, up_all, back_up, proj,
    local_sem, recv, sib_recv, z_send, y_send, x_send, sib_send,
    halo_send, halo_recv, down_send, down_recv, up_send, up_recv,
):
    f, c = lax.axis_index("fsdp"), lax.axis_index("ctx")
    n_f, n_c = up_all.shape[0], 2 * line
    tile = pl.program_id(0)
    last = pl.num_programs(0) - 1
    x, k, z, y = f // 2, f % 2, c // 2, c % 2
    half = own_ref.shape[0] // 2
    x_peer = (lax.rem(f + 2, 4), c)
    sibling = (f + 1 - 2 * k, c)
    y_peer = (f, c + 1 - 2 * y)
    z_up, z_down = (f, c + 2), (f, c - 2)

    def place(h, xx, yy, zz, kk):
        rows = pl.ds((2 * zz + yy) * (2 * half) + h * half, half)
        return all_ref.at[2 * xx + kk, rows, :]

    def copy(h, xx, yy, zz, send, arrive, to):
        block = place(h, xx, yy, zz, k)
        return pltpu.make_async_remote_copy(
            src_ref=block, dst_ref=block, send_sem=send, recv_sem=arrive,
            device_id=to, device_id_type=MESH,
        )

    def along_x(h, xx, yy, zz):
        return copy(h, xx, yy, zz, x_send.at[h, xx, yy, zz], recv.at[h, xx, yy, zz], x_peer)

    def along_y(h, xx, yy, zz):
        return copy(h, xx, yy, zz, y_send.at[h, xx, yy, zz], recv.at[h, xx, yy, zz], y_peer)

    def along_z(h, zz, up):
        return copy(
            h, x, y, zz, z_send.at[h, up, zz], recv.at[h, x, y, zz], z_up if up else z_down
        )

    def to_sibling(h, xx, yy, zz):
        return copy(h, xx, yy, zz, sib_send.at[h, xx, yy, zz], sib_recv.at[h, xx, yy, zz], sibling)

    def arrived(h, xx, yy, zz):
        along_x(h, xx, yy, zz).wait_recv()

    def places(step):
        yield z - step, z - step >= 0, True
        if step:
            yield z + step, z + step < line, False

    def first(step):
        for zz, there, upward in places(step):
            @pl.when(there)
            def _():
                for h in (0, 1):
                    if step:
                        arrived(h, x, y, zz)
                    if upward:
                        @pl.when(z + 1 < line)
                        def _():
                            along_z(h, zz, 1).start()
                    if not upward or step == 0:
                        @pl.when(z > 0)
                        def _():
                            along_z(h, zz, 0).start()
                for h in (0, 1):
                    along_y(h, x, y, zz).start()
                    along_x(1 - h, x, y, zz).start()
                for h in (0, 1):
                    to_sibling(h, x, y, zz).start()

    def second(step):
        for zz, there, _ in places(step):
            @pl.when(there)
            def _():
                arrived(0, x, 1 - y, zz)
                along_x(0, x, 1 - y, zz).start()
                arrived(1, 1 - x, y, zz)
                along_y(1, 1 - x, y, zz).start()
                to_sibling(0, x, 1 - y, zz).start()
                to_sibling(1, 1 - x, y, zz).start()

    def third(step):
        for zz, there, _ in places(step):
            @pl.when(there)
            def _():
                for other in (y, 1 - y):
                    arrived(0, 1 - x, other, zz)
                    to_sibling(0, 1 - x, other, zz).start()
                for other in (x, 1 - x):
                    arrived(1, other, 1 - y, zz)
                    to_sibling(1, other, 1 - y, zz).start()

    own_rows = down_ref.shape[0]

    def halo():
        return pltpu.make_async_remote_copy(
            src_ref=tail_ref, dst_ref=before, send_sem=halo_send, recv_sem=halo_recv,
            device_id=(f, c + 1), device_id_type=MESH,
        )

    def down_copy(turn, origin):
        return pltpu.make_async_remote_copy(
            src_ref=down_ref, dst_ref=down_all.at[pl.ds(origin * own_rows, own_rows)],
            send_sem=down_send.at[turn], recv_sem=down_recv.at[origin],
            device_id=(f, lax.rem(c + turn, n_c)), device_id_type=MESH,
        )

    def up_copy(turn, origin):
        return pltpu.make_async_remote_copy(
            src_ref=up_ref, dst_ref=up_all.at[origin],
            send_sem=up_send.at[turn], recv_sem=up_recv.at[origin],
            device_id=(lax.rem(f + turn, n_f), c), device_id_type=MESH,
        )

    def advance(step):
        if step < line:
            first(step)
        if 1 <= step <= line:
            second(step - 1)
        if step >= 2:
            third(step - 2)

    nt = (((1,), (1,)), ((), ()))
    over_rows = (((0,), (0,)), ((), ()))

    @pl.when(tile == 0)
    def _():
        mine = pltpu.make_async_copy(
            own_ref, all_ref.at[f, pl.ds(c * (2 * half), 2 * half), :], local_sem
        )
        mine.start()
        barrier = pltpu.get_barrier_semaphore()
        for turn in range(1, n_c):
            pl.semaphore_signal(
                barrier, inc=1, device_id=(f, lax.rem(c + turn, n_c)), device_id_type=MESH
            )
        for turn in range(1, n_f):
            pl.semaphore_signal(
                barrier, inc=1, device_id=(lax.rem(f + turn, n_f), c), device_id_type=MESH
            )
        pl.semaphore_wait(barrier, n_c + n_f - 2)

        @pl.when(c + 1 < n_c)
        def _():
            halo().start()

        for turn in range(1, n_f):
            up_copy(turn, f).start()
        for turn in range(1, n_c):
            down_copy(turn, c).start()
        mine.wait()
        advance(0)
        up_all[f] = up_ref[...]
        down_all[pl.ds(pl.multiple_of(c * own_rows, own_rows), own_rows)] = down_ref[...]
        proj[...] = jnp.zeros_like(proj)
        for turn in range(1, n_f):
            up_copy(turn, lax.rem(f + turn, n_f)).wait_recv()
        for turn in range(1, n_c):
            down_copy(turn, lax.rem(c + turn, n_c)).wait_recv()
        width = up_ref.shape[1]
        partial = jnp.zeros(proj.shape, jnp.float32)
        for g in range(n_f):
            columns = slice(g * width, (g + 1) * width)
            up_out[:, columns] = up_all[g]
            partial = partial + lax.dot_general(
                cot_ref[:, columns], up_all[g], nt, preferred_element_type=jnp.float32
            )
        back_up[...] = partial.astype(jnp.bfloat16)
        back_up_ref[...] = partial.astype(jnp.bfloat16)
        down_out[...] = down_all[...]

        @pl.when(c > 0)
        def _():
            halo().wait_recv()

        @pl.when(c == 0)
        def _():
            before[...] = jnp.zeros_like(before)

    for step, when in ((1, 2), (2, 16)):
        @pl.when(tile == when)
        def _():
            advance(step)

    taps = base_ref.shape[1] // 2
    lanes = pl.ds(pl.multiple_of(tile * LANES, LANES), LANES)
    mixed = (key_ref[...].astype(jnp.float32) * value_ref[...].astype(jnp.float32)).astype(
        jnp.bfloat16
    )
    joined = jnp.concatenate([before[:, lanes], mixed], 0)
    windows = [joined[b * taps : (b + 2) * taps] for b in range(mixed.shape[0] // taps)]
    gated = conv_blocks(base_ref[...], windows) + skip_ref[...] * mixed.astype(jnp.float32)
    gated_ref[...] = gated
    gated_input = (query_ref[...].astype(jnp.float32) * gated).astype(jnp.bfloat16)
    input_ref[...] = gated_input
    proj[...] += jnp.dot(gated_input, down_all[lanes], preferred_element_type=jnp.float32)
    term_down_ref[...] = lax.dot_general(
        gated_input, back_up[...], over_rows, preferred_element_type=jnp.float32
    )

    def finish(zz, carry):
        for xx in (0, 1):
            for yy in (0, 1):
                for h in (0, 1):
                    to_sibling(h, xx, yy, zz).wait()
        for yy in (0, 1):
            along_x(0, x, yy, zz).wait_send()
        along_x(1, x, y, zz).wait_send()
        for xx in (0, 1):
            along_y(1, xx, y, zz).wait_send()
        along_y(0, x, y, zz).wait_send()
        for h in (0, 1):
            @pl.when(jnp.logical_and(zz <= z, z + 1 < line))
            def _():
                along_z(h, zz, 1).wait_send()

            @pl.when(jnp.logical_and(zz >= z, z > 0))
            def _():
                along_z(h, zz, 0).wait_send()
        return carry

    @pl.when(tile == last)
    def _():
        rounded = proj[...].astype(jnp.bfloat16)
        proj_ref[...] = rounded
        term_up_ref[...] = lax.dot_general(
            rounded, cot_ref[...], over_rows, preferred_element_type=jnp.float32
        )
        for step in range(3, line + 2):
            advance(step)
        lax.fori_loop(0, line, finish, 0)
        for turn in range(1, n_f):
            up_copy(turn, f).wait_send()
        for turn in range(1, n_c):
            down_copy(turn, c).wait_send()

        @pl.when(c + 1 < n_c)
        def _():
            halo().wait_send()


def gather_weight(tail, piece, down, up, cot, query, key, value, base, skip, n_f, n_c):
    rows, columns = piece.shape
    line = n_c // 2
    blocks = (2, 2, 2, line)
    count, channels = query.shape
    rank, width = up.shape
    tiles = channels // LANES
    held = pl.BlockSpec(memory_space=pltpu.VMEM)
    tile = pl.BlockSpec((count, LANES), lambda i: (0, i))
    whole = lambda *shape: pl.BlockSpec(shape, lambda i: (0, 0))
    shape = jax.ShapeDtypeStruct
    half = jnp.bfloat16
    full = jnp.float32
    return pl.pallas_call(
        functools.partial(gather_kernel, line),
        grid=(tiles,),
        out_shape=[
            shape((n_f, n_c * rows, columns), half),
            shape((count, channels), full),
            shape((count, channels), half),
            shape((channels, rank), full),
            shape((rank, n_f * width), full),
            shape((count, rank), half),
            shape((count, rank), half),
            shape((channels, rank), half),
            shape((rank, n_f * width), half),
        ],
        in_specs=[
            held,
            pl.BlockSpec(memory_space=pl.ANY),
            held,
            held,
            whole(*cot.shape),
            tile,
            tile,
            tile,
            pl.BlockSpec((base.shape[0] // tiles, base.shape[1]), lambda i: (i, 0)),
            pl.BlockSpec((1, LANES), lambda i: (0, i)),
        ],
        out_specs=[
            pl.BlockSpec(memory_space=pl.ANY),
            tile,
            tile,
            pl.BlockSpec((LANES, rank), lambda i: (i, 0)),
            whole(rank, n_f * width),
            whole(count, rank),
            whole(count, rank),
            whole(channels, rank),
            whole(rank, n_f * width),
        ],
        scratch_shapes=[
            pltpu.VMEM(tail.shape, half),
            pltpu.VMEM((channels, rank), half),
            pltpu.VMEM((n_f, rank, width), half),
            pltpu.VMEM((count, rank), half),
            pltpu.VMEM((count, rank), full),
            pltpu.SemaphoreType.DMA,
            pltpu.SemaphoreType.DMA(blocks),
            pltpu.SemaphoreType.DMA(blocks),
            pltpu.SemaphoreType.DMA((2, 2, line)),
            pltpu.SemaphoreType.DMA(blocks),
            pltpu.SemaphoreType.DMA(blocks),
            pltpu.SemaphoreType.DMA(blocks),
            pltpu.SemaphoreType.DMA,
            pltpu.SemaphoreType.DMA,
            pltpu.SemaphoreType.DMA((n_c,)),
            pltpu.SemaphoreType.DMA((n_c,)),
            pltpu.SemaphoreType.DMA((n_f,)),
            pltpu.SemaphoreType.DMA((n_f,)),
        ],
        compiler_params=pltpu.CompilerParams(
            collective_id=0, has_side_effects=True, vmem_limit_bytes=VMEM_LIMIT
        ),
        cost_estimate=pl.CostEstimate(
            flops=0, bytes_accessed=16 * n_f * n_c * rows * columns, transcendentals=0
        ),
        name="gather_weight",
    )(tail, piece, down, up, cot, query, key, value, base, skip)


def conv_blocks(base, windows):
    filters_here, width = base.shape
    taps = width // 2
    toep = jnp.concatenate(
        [
            pltpu.roll(
                jnp.broadcast_to(base[g : g + 1], (taps, width)), 0, 1, stride=1, stride_axis=0
            )
            for g in range(filters_here)
        ],
        0,
    ).astype(jnp.bfloat16)
    product = jnp.dot(toep, jnp.concatenate(windows, 1), preferred_element_type=jnp.float32)
    lanes = lax.broadcasted_iota(jnp.int32, (taps, LANES), 1) // (LANES // filters_here)
    results = []
    for b in range(len(windows)):
        part = product[:, b * LANES : (b + 1) * LANES]
        chosen = part[:taps]
        for g in range(1, filters_here):
            chosen = jnp.where(lanes == g, part[g * taps : (g + 1) * taps], chosen)
        results.append(chosen)
    return jnp.concatenate(results, 0)


def back_kernel(grad_ref, after_ref, key_ref, value_ref, base_ref, skip_ref, gk_ref, gv_ref):
    taps = base_ref.shape[1] // 2
    grad = grad_ref[...]
    joined = jnp.concatenate([grad, after_ref[...]], 0)
    windows = [joined[b * taps : (b + 2) * taps] for b in range(grad.shape[0] // taps)]
    grad_mixed = conv_blocks(base_ref[...], windows) + skip_ref[...] * grad.astype(jnp.float32)
    gk_ref[...] = (grad_mixed * value_ref[...].astype(jnp.float32)).astype(jnp.bfloat16)
    gv_ref[...] = (grad_mixed * key_ref[...].astype(jnp.float32)).astype(jnp.bfloat16)


def tile_call(kernel, operands, out_types, groups, name):
    rows, channels = operands[0].shape
    tiles = channels // LANES

    def spec(array):
        if array.shape[0] == groups:
            if array.shape[1] != channels:
                return pl.BlockSpec((groups // tiles, array.shape[1]), lambda i: (i, 0))
        return pl.BlockSpec((array.shape[0], LANES), lambda i: (0, i))

    return pl.pallas_call(
        kernel,
        grid=(tiles,),
        in_specs=[spec(a) for a in operands],
        out_specs=[pl.BlockSpec((rows, LANES), lambda i: (0, i)) for _ in out_types],
        out_shape=[jax.ShapeDtypeStruct((rows, channels), t) for t in out_types],
        compiler_params=pltpu.CompilerParams(vmem_limit_bytes=VMEM_LIMIT),
        cost_estimate=pl.CostEstimate(
            flops=rows * channels * 4096, bytes_accessed=rows * channels * 12, transcendentals=0
        ),
        name=name,
    )(*operands)


def product_kernel(
    weight_ref, cot_ref, input_ref, gated_ref, query_ref, back_up_ref, down_ref, proj_ref, up_ref,
    out_ref, gq_ref, gg_ref, total,
):
    step = pl.program_id(0)
    parts, _, width = weight_ref.shape

    @pl.when(step == 0)
    def _():
        total[...] = adapter_scale * jnp.dot(
            proj_ref[...], up_ref[...], preferred_element_type=jnp.float32
        )

    nt = (((1,), (1,)), ((), ()))
    back = adapter_scale * lax.dot_general(
        back_up_ref[...], down_ref[...], nt, preferred_element_type=jnp.float32
    )
    for f in range(parts):
        columns = slice(f * width, (f + 1) * width)
        weight = weight_ref[f]
        back = back + lax.dot_general(
            cot_ref[:, columns], weight, nt, preferred_element_type=jnp.float32
        )
        total[:, columns] += jnp.dot(input_ref[...], weight, preferred_element_type=jnp.float32)
    gq_ref[...] = (back * gated_ref[...]).astype(jnp.bfloat16)
    gg_ref[...] = (back * query_ref[...].astype(jnp.float32)).astype(jnp.bfloat16)

    @pl.when(step == pl.num_programs(0) - 1)
    def _():
        out_ref[...] = total[...].astype(jnp.bfloat16)


def products(weight, cot, gated_input, gated, query, back_up, down, proj, up):
    parts, channels, width = weight.shape
    rows = cot.shape[0]
    features = parts * width
    rank = down.shape[1]
    block = 512
    whole = lambda i: (0, 0)
    tile = pl.BlockSpec((rows, block), lambda i: (0, i))
    return pl.pallas_call(
        product_kernel,
        grid=(channels // block,),
        in_specs=[
            pl.BlockSpec((parts, block, width), lambda i: (0, i, 0)),
            pl.BlockSpec((rows, features), whole),
            tile,
            tile,
            tile,
            pl.BlockSpec((rows, rank), whole),
            pl.BlockSpec((block, rank), lambda i: (i, 0)),
            pl.BlockSpec((rows, rank), whole),
            pl.BlockSpec((rank, features), whole),
        ],
        out_specs=[pl.BlockSpec((rows, features), whole), tile, tile],
        out_shape=[
            jax.ShapeDtypeStruct((rows, features), jnp.bfloat16),
            jax.ShapeDtypeStruct((rows, channels), jnp.bfloat16),
            jax.ShapeDtypeStruct((rows, channels), jnp.bfloat16),
        ],
        scratch_shapes=[pltpu.VMEM((rows, features), jnp.float32)],
        compiler_params=pltpu.CompilerParams(vmem_limit_bytes=VMEM_LIMIT),
        cost_estimate=pl.CostEstimate(
            flops=4 * rows * channels * features,
            bytes_accessed=2 * channels * features,
            transcendentals=0,
        ),
        name="products",
    )(weight, cot, gated_input, gated, query, back_up, down, proj, up)


def local(
    query_branch,
    key_branch,
    value_branch,
    cotangent,
    quantized_weight_codes,
    scale_code_bytes,
    row_scale_second,
    filters,
    channel_skip_weight,
    adapter_down_weight,
    adapter_up_weight,
):
    groups, filter_len = filters.shape
    query, key, value, cot = query_branch[0], key_branch[0], value_branch[0], cotangent[0]
    row_count = query.shape[0]
    n_f, n_c = lax.axis_size("fsdp"), lax.axis_size("ctx")
    token_count = query_branch.shape[0] * row_count * n_c * n_f
    multiplier = adapter_scale / math.sqrt(token_count)
    skip = channel_skip_weight[None]

    tail = row_count - filter_len
    mixed_tail = (
        key[tail:].astype(jnp.float32) * value[tail:].astype(jnp.float32)
    ).astype(jnp.bfloat16)
    piece = dequantize(quantized_weight_codes, scale_code_bytes, row_scale_second)
    taps = filters.astype(jnp.float32)
    zeros = jnp.zeros((groups, filter_len), jnp.float32)
    back_base = jnp.concatenate([taps, zeros], 1)
    ahead_base = jnp.concatenate([zeros[:, :1], jnp.flip(taps, 1), zeros[:, 1:]], 1)

    weight, gated, gated_input, term_down, term_up, proj, back_up, down, up = gather_weight(
        mixed_tail, piece, adapter_down_weight, adapter_up_weight, cot, query, key, value,
        ahead_base, skip, n_f, n_c,
    )
    part_up = lax.psum_scatter(term_up, "fsdp", scatter_dimension=1, tiled=True)
    part_down = lax.psum_scatter(term_down, "ctx", scatter_dimension=0, tiled=True)
    grad_down = multiplier * lax.psum(part_down, "fsdp")
    part_up = lax.psum_scatter(part_up, "ctx", scatter_dimension=0, tiled=True)
    grad_up = lax.all_gather(
        (multiplier * part_up).astype(jnp.bfloat16), "ctx", axis=0, tiled=True
    )

    output, grad_query, grad_gated = products(
        weight, cot, gated_input, gated, query, back_up, down, proj, up
    )
    after = from_behind(grad_gated[:filter_len], "ctx", -1)
    grad_key, grad_value = tile_call(
        back_kernel,
        (grad_gated, after, key, value, back_base, skip),
        (jnp.bfloat16, jnp.bfloat16),
        groups,
        "conv_back",
    )
    return (
        output[None],
        grad_query[None],
        grad_key[None],
        grad_value[None],
        grad_down.astype(jnp.bfloat16),
        grad_up.astype(jnp.bfloat16),
    )


def solution(mesh):
    return jax.shard_map(
        local,
        mesh=mesh,
        in_specs=(
            P("fsdp", "ctx", None),
            P("fsdp", "ctx", None),
            P("fsdp", "ctx", None),
            P("fsdp", "ctx", None),
            P("ctx", "fsdp"),
            P("ctx", "fsdp"),
            P("ctx"),
            P(),
            P(),
            P("ctx", None),
            P(None, "fsdp"),
        ),
        out_specs=(
            P("fsdp", "ctx", None),
            P("fsdp", "ctx", None),
            P("fsdp", "ctx", None),
            P("fsdp", "ctx", None),
            P("ctx", None),
            P(None, "fsdp"),
        ),
        check_vma=False,
    )
```

```python
import functools
import math

import jax
import jax.numpy as jnp
from jax import lax
from jax.experimental import pallas as pl
from jax.experimental.pallas import tpu as pltpu
from jax.sharding import PartitionSpec as P

QBLOCK = 64
LANES = 128
MESH = pl.DeviceIdType.MESH
VMEM_LIMIT = 56 * 1024 * 1024

normal_levels = (
    -1.0,
    -0.6961928009986877,
    -0.5250730514526367,
    -0.39491748809814453,
    -0.28444138169288635,
    -0.18477343022823334,
    -0.09105003625154495,
    0.0,
    0.07958029955625534,
    0.16093020141124725,
    0.24611230194568634,
    0.33791524171829224,
    0.44070982933044434,
    0.5626170039176941,
    0.7229568362236023,
    1.0,
)
adapter_scale = 0.25


def from_behind(shard, axis, by):
    count = lax.axis_size(axis)
    pairs = [(i, i + by) for i in range(count) if 0 <= i + by < count]
    return lax.ppermute(shard, axis, pairs)


def dequantize(quantized_weight_codes, scale_code_bytes, row_scale_second):
    levels = jnp.zeros(quantized_weight_codes.shape, jnp.float32)
    for number in range(16):
        levels = jnp.where(quantized_weight_codes == number, normal_levels[number], levels)
    absmax = row_scale_second[:, None] * (scale_code_bytes.astype(jnp.float32) + 1.0) / 256.0
    absmax = jnp.repeat(absmax, QBLOCK, axis=1)
    return (levels * absmax).astype(jnp.bfloat16)


def gather_kernel(
    line, multiplier, tail_ref, own_ref, down_ref, up_ref, cot_ref, query_ref, key_ref, value_ref, base_ref, skip_ref, back_base_ref,
    all_ref, gated_ref, input_ref, grad_down_ref, grad_up_ref, proj_ref, back_up_ref, down_out, up_out, toep_ref,
    before, down_all, up_all, back_up, proj,
    term_down, term_up, down_parts, up_parts, down_sum, down_sums, up_pieces, up_sums, up_whole,
    local_sem, recv, sib_recv, z_send, y_send, x_send, sib_send,
    halo_send, halo_recv, down_send, down_recv, up_send, up_recv,
    send_1, recv_1, send_2, recv_2, send_3, recv_3, send_4, recv_4, send_5, recv_5,
):
    f, c = lax.axis_index("fsdp"), lax.axis_index("ctx")
    n_f, n_c = up_all.shape[0], 2 * line
    tile = pl.program_id(0)
    last = pl.num_programs(0) - 1
    x, k, z, y = f // 2, f % 2, c // 2, c % 2
    half = own_ref.shape[0] // 2
    x_peer = (lax.rem(f + 2, 4), c)
    sibling = (f + 1 - 2 * k, c)
    y_peer = (f, c + 1 - 2 * y)
    z_up, z_down = (f, c + 2), (f, c - 2)

    def place(h, xx, yy, zz, kk):
        rows = pl.ds((2 * zz + yy) * (2 * half) + h * half, half)
        return all_ref.at[2 * xx + kk, rows, :]

    def copy(h, xx, yy, zz, send, arrive, to):
        block = place(h, xx, yy, zz, k)
        return pltpu.make_async_remote_copy(
            src_ref=block, dst_ref=block, send_sem=send, recv_sem=arrive,
            device_id=to, device_id_type=MESH,
        )

    def along_x(h, xx, yy, zz):
        return copy(h, xx, yy, zz, x_send.at[h, xx, yy, zz], recv.at[h, xx, yy, zz], x_peer)

    def along_y(h, xx, yy, zz):
        return copy(h, xx, yy, zz, y_send.at[h, xx, yy, zz], recv.at[h, xx, yy, zz], y_peer)

    def along_z(h, zz, up):
        return copy(
            h, x, y, zz, z_send.at[h, up, zz], recv.at[h, x, y, zz], z_up if up else z_down
        )

    def to_sibling(h, xx, yy, zz):
        return copy(h, xx, yy, zz, sib_send.at[h, xx, yy, zz], sib_recv.at[h, xx, yy, zz], sibling)

    def arrived(h, xx, yy, zz):
        along_x(h, xx, yy, zz).wait_recv()

    def places(step):
        yield z - step, z - step >= 0, True
        if step:
            yield z + step, z + step < line, False

    def first(step):
        for zz, there, upward in places(step):
            @pl.when(there)
            def _():
                for h in (0, 1):
                    if step:
                        arrived(h, x, y, zz)
                    if upward:
                        @pl.when(z + 1 < line)
                        def _():
                            along_z(h, zz, 1).start()
                    if not upward or step == 0:
                        @pl.when(z > 0)
                        def _():
                            along_z(h, zz, 0).start()
                for h in (0, 1):
                    along_y(h, x, y, zz).start()
                    along_x(1 - h, x, y, zz).start()
                for h in (0, 1):
                    to_sibling(h, x, y, zz).start()

    def second(step):
        for zz, there, _ in places(step):
            @pl.when(there)
            def _():
                arrived(0, x, 1 - y, zz)
                along_x(0, x, 1 - y, zz).start()
                arrived(1, 1 - x, y, zz)
                along_y(1, 1 - x, y, zz).start()
                to_sibling(0, x, 1 - y, zz).start()
                to_sibling(1, 1 - x, y, zz).start()

    def third(step):
        for zz, there, _ in places(step):
            @pl.when(there)
            def _():
                for other in (y, 1 - y):
                    arrived(0, 1 - x, other, zz)
                    to_sibling(0, 1 - x, other, zz).start()
                for other in (x, 1 - x):
                    arrived(1, other, 1 - y, zz)
                    to_sibling(1, other, 1 - y, zz).start()

    own_rows = down_ref.shape[0]

    def halo():
        return pltpu.make_async_remote_copy(
            src_ref=tail_ref, dst_ref=before, send_sem=halo_send, recv_sem=halo_recv,
            device_id=(f, c + 1), device_id_type=MESH,
        )

    def down_copy(turn, origin):
        return pltpu.make_async_remote_copy(
            src_ref=down_ref, dst_ref=down_all.at[pl.ds(origin * own_rows, own_rows)],
            send_sem=down_send.at[turn], recv_sem=down_recv.at[origin],
            device_id=(f, lax.rem(c + turn, n_c)), device_id_type=MESH,
        )

    def up_copy(turn, origin):
        return pltpu.make_async_remote_copy(
            src_ref=up_ref, dst_ref=up_all.at[origin],
            send_sem=up_send.at[turn], recv_sem=up_recv.at[origin],
            device_id=(lax.rem(f + turn, n_f), c), device_id_type=MESH,
        )

    def pushes(on_ctx, source, target, send, arrive, incoming=False):
        count, me = (n_c, c) if on_ctx else (n_f, f)
        for turn in range(1, count):
            peer = lax.rem(me + turn, count)
            origin = peer if incoming else me
            yield pltpu.make_async_remote_copy(
                src_ref=source(peer), dst_ref=target.at[origin],
                send_sem=send.at[turn], recv_sem=arrive.at[origin],
                device_id=(f, peer) if on_ctx else (peer, c), device_id_type=MESH,
            )

    def rows_of(peer):
        return term_down.at[pl.ds(pl.multiple_of(peer * own_rows, own_rows), own_rows)]

    sums = (
        (True, rows_of, down_parts, send_1, recv_1),
        (False, lambda peer: term_up.at[peer], up_parts, send_2, recv_2),
        (False, lambda peer: down_sum, down_sums, send_3, recv_3),
        (True, lambda peer: up_pieces.at[peer], up_sums, send_4, recv_4),
        (True, lambda peer: up_whole.at[c], up_whole, send_5, recv_5),
    )

    def begin(number):
        for push in pushes(*sums[number]):
            push.start()

    def await_parts(number):
        for push in pushes(*sums[number], incoming=True):
            push.wait_recv()

    def total_of(parts):
        result = parts[0]
        for number in range(1, parts.shape[0]):
            result = result + parts[number]
        return result

    def advance(step):
        if step < line:
            first(step)
        if 1 <= step <= line:
            second(step - 1)
        if step >= 2:
            third(step - 2)

    nt = (((1,), (1,)), ((), ()))
    over_rows = (((0,), (0,)), ((), ()))

    @pl.when(tile == 0)
    def _():
        mine = pltpu.make_async_copy(
            own_ref, all_ref.at[f, pl.ds(c * (2 * half), 2 * half), :], local_sem
        )
        mine.start()
        barrier = pltpu.get_barrier_semaphore()
        for turn in range(1, n_c):
            pl.semaphore_signal(
                barrier, inc=1, device_id=(f, lax.rem(c + turn, n_c)), device_id_type=MESH
            )
        for turn in range(1, n_f):
            pl.semaphore_signal(
                barrier, inc=1, device_id=(lax.rem(f + turn, n_f), c), device_id_type=MESH
            )
        pl.semaphore_wait(barrier, n_c + n_f - 2)

        @pl.when(c + 1 < n_c)
        def _():
            halo().start()

        for turn in range(1, n_f):
            up_copy(turn, f).start()
        for turn in range(1, n_c):
            down_copy(turn, c).start()
        mine.wait()
        advance(0)
        up_all[f] = up_ref[...]
        down_all[pl.ds(pl.multiple_of(c * own_rows, own_rows), own_rows)] = down_ref[...]
        proj[...] = jnp.zeros_like(proj)
        for turn in range(1, n_f):
            up_copy(turn, lax.rem(f + turn, n_f)).wait_recv()
        for turn in range(1, n_c):
            down_copy(turn, lax.rem(c + turn, n_c)).wait_recv()
        width = up_ref.shape[1]
        partial = jnp.zeros(proj.shape, jnp.float32)
        for g in range(n_f):
            columns = slice(g * width, (g + 1) * width)
            up_out[:, columns] = up_all[g]
            partial = partial + lax.dot_general(
                cot_ref[:, columns], up_all[g], nt, preferred_element_type=jnp.float32
            )
        back_up[...] = partial.astype(jnp.bfloat16)
        back_up_ref[...] = partial.astype(jnp.bfloat16)
        down_out[...] = down_all[...]

        @pl.when(c > 0)
        def _():
            halo().wait_recv()

        @pl.when(c == 0)
        def _():
            before[...] = jnp.zeros_like(before)

    for step, when in ((1, 2), (2, 16)):
        @pl.when(tile == when)
        def _():
            advance(step)

    toep_ref[...] = toeplitz(back_base_ref[...])
    taps = base_ref.shape[1] // 2
    lanes = pl.ds(pl.multiple_of(tile * LANES, LANES), LANES)
    mixed = (key_ref[...].astype(jnp.float32) * value_ref[...].astype(jnp.float32)).astype(
        jnp.bfloat16
    )
    joined = jnp.concatenate([before[:, lanes], mixed], 0)
    windows = [joined[b * taps : (b + 2) * taps] for b in range(mixed.shape[0] // taps)]
    gated = conv_blocks(toeplitz(base_ref[...]), windows) + skip_ref[...] * mixed.astype(jnp.float32)
    gated_ref[...] = gated
    gated_input = (query_ref[...].astype(jnp.float32) * gated).astype(jnp.bfloat16)
    input_ref[...] = gated_input
    proj[...] += jnp.dot(gated_input, down_all[lanes], preferred_element_type=jnp.float32)
    term_down[lanes] = lax.dot_general(
        gated_input, back_up[...], over_rows, preferred_element_type=jnp.float32
    )

    def finish(zz, carry):
        for xx in (0, 1):
            for yy in (0, 1):
                for h in (0, 1):
                    to_sibling(h, xx, yy, zz).wait()
        for yy in (0, 1):
            along_x(0, x, yy, zz).wait_send()
        along_x(1, x, y, zz).wait_send()
        for xx in (0, 1):
            along_y(1, xx, y, zz).wait_send()
        along_y(0, x, y, zz).wait_send()
        for h in (0, 1):
            @pl.when(jnp.logical_and(zz <= z, z + 1 < line))
            def _():
                along_z(h, zz, 1).wait_send()

            @pl.when(jnp.logical_and(zz >= z, z > 0))
            def _():
                along_z(h, zz, 0).wait_send()
        return carry

    @pl.when(tile == last)
    def _():
        rounded = proj[...].astype(jnp.bfloat16)
        proj_ref[...] = rounded
        width = up_ref.shape[1]
        for g in range(n_f):
            term_up[g] = lax.dot_general(
                rounded, cot_ref[:, g * width : (g + 1) * width], over_rows,
                preferred_element_type=jnp.float32,
            )
        begin(0)
        begin(1)
        down_parts[c] = rows_of(c)[...]
        up_parts[f] = term_up[f]
        advance(3)
        await_parts(0)
        await_parts(1)
        down_sum[...] = total_of(down_parts)
        down_sums[f] = down_sum[...]
        up_mine = total_of(up_parts)
        piece = up_mine.shape[0] // n_c
        for g in range(n_c):
            up_pieces[g] = up_mine[g * piece : (g + 1) * piece]
        begin(2)
        begin(3)
        up_sums[c] = up_pieces[c]
        for step in range(4, line + 1):
            advance(step)
        await_parts(2)
        await_parts(3)
        grad_down_ref[...] = (multiplier * total_of(down_sums)).astype(jnp.bfloat16)
        up_whole[c] = multiplier * total_of(up_sums)
        begin(4)
        advance(line + 1)
        await_parts(4)
        grad_up_ref[...] = jnp.concatenate(
            [up_whole[g] for g in range(n_c)], 0
        ).astype(jnp.bfloat16)
        for group in sums:
            for push in pushes(*group):
                push.wait_send()
        lax.fori_loop(0, line, finish, 0)
        for turn in range(1, n_f):
            up_copy(turn, f).wait_send()
        for turn in range(1, n_c):
            down_copy(turn, c).wait_send()

        @pl.when(c + 1 < n_c)
        def _():
            halo().wait_send()


def gather_weight(tail, piece, down, up, cot, query, key, value, base, skip, back_base, n_f, n_c, multiplier):
    rows, columns = piece.shape
    line = n_c // 2
    blocks = (2, 2, 2, line)
    count, channels = query.shape
    rank, width = up.shape
    tiles = channels // LANES
    held = pl.BlockSpec(memory_space=pltpu.VMEM)
    tile = pl.BlockSpec((count, LANES), lambda i: (0, i))
    whole = lambda *shape: pl.BlockSpec(shape, lambda i: (0, 0))
    shape = jax.ShapeDtypeStruct
    half = jnp.bfloat16
    full = jnp.float32
    return pl.pallas_call(
        functools.partial(gather_kernel, line, multiplier),
        grid=(tiles,),
        out_shape=[
            shape((n_f, n_c * rows, columns), half),
            shape((count, channels), full),
            shape((count, channels), half),
            shape((rows, rank), half),
            shape((rank, width), half),
            shape((count, rank), half),
            shape((count, rank), half),
            shape((channels, rank), half),
            shape((rank, n_f * width), half),
            shape((base.shape[0] * base.shape[1] // 2, base.shape[1]), half),
        ],
        in_specs=[
            held,
            pl.BlockSpec(memory_space=pl.ANY),
            held,
            held,
            whole(*cot.shape),
            tile,
            tile,
            tile,
            pl.BlockSpec((base.shape[0] // tiles, base.shape[1]), lambda i: (i, 0)),
            pl.BlockSpec((1, LANES), lambda i: (0, i)),
            pl.BlockSpec((base.shape[0] // tiles, base.shape[1]), lambda i: (i, 0)),
        ],
        out_specs=[
            pl.BlockSpec(memory_space=pl.ANY),
            tile,
            tile,
            whole(rows, rank),
            whole(rank, width),
            whole(count, rank),
            whole(count, rank),
            whole(channels, rank),
            whole(rank, n_f * width),
            pl.BlockSpec(
                (base.shape[0] // tiles * base.shape[1] // 2, base.shape[1]), lambda i: (i, 0)
            ),
        ],
        scratch_shapes=[
            pltpu.VMEM(tail.shape, half),
            pltpu.VMEM((channels, rank), half),
            pltpu.VMEM((n_f, rank, width), half),
            pltpu.VMEM((count, rank), half),
            pltpu.VMEM((count, rank), full),
            pltpu.VMEM((channels, rank), full),
            pltpu.VMEM((n_f, rank, width), full),
            pltpu.VMEM((n_c, rows, rank), full),
            pltpu.VMEM((n_f, rank, width), full),
            pltpu.VMEM((rows, rank), full),
            pltpu.VMEM((n_f, rows, rank), full),
            pltpu.VMEM((n_c, rank // n_c, width), full),
            pltpu.VMEM((n_c, rank // n_c, width), full),
            pltpu.VMEM((n_c, rank // n_c, width), full),
            pltpu.SemaphoreType.DMA,
            pltpu.SemaphoreType.DMA(blocks),
            pltpu.SemaphoreType.DMA(blocks),
            pltpu.SemaphoreType.DMA((2, 2, line)),
            pltpu.SemaphoreType.DMA(blocks),
            pltpu.SemaphoreType.DMA(blocks),
            pltpu.SemaphoreType.DMA(blocks),
            pltpu.SemaphoreType.DMA,
            pltpu.SemaphoreType.DMA,
            pltpu.SemaphoreType.DMA((n_c,)),
            pltpu.SemaphoreType.DMA((n_c,)),
            pltpu.SemaphoreType.DMA((n_f,)),
            pltpu.SemaphoreType.DMA((n_f,)),
        ]
        + [pltpu.SemaphoreType.DMA((n,)) for n in (n_c, n_f, n_f, n_c, n_c) for _ in range(2)],
        compiler_params=pltpu.CompilerParams(
            collective_id=0, has_side_effects=True, vmem_limit_bytes=VMEM_LIMIT
        ),
        cost_estimate=pl.CostEstimate(
            flops=0, bytes_accessed=16 * n_f * n_c * rows * columns, transcendentals=0
        ),
        name="gather_weight",
    )(tail, piece, down, up, cot, query, key, value, base, skip, back_base)


def toeplitz(base):
    taps = base.shape[1] // 2
    return jnp.concatenate(
        [
            pltpu.roll(
                jnp.broadcast_to(base[g : g + 1], (taps, 2 * taps)), 0, 1, stride=1, stride_axis=0
            )
            for g in range(base.shape[0])
        ],
        0,
    ).astype(jnp.bfloat16)


def conv_blocks(toep, windows):
    taps = toep.shape[1] // 2
    filters_here = toep.shape[0] // taps
    product = jnp.dot(toep, jnp.concatenate(windows, 1), preferred_element_type=jnp.float32)
    lanes = lax.broadcasted_iota(jnp.int32, (taps, LANES), 1) // (LANES // filters_here)
    results = []
    for b in range(len(windows)):
        part = product[:, b * LANES : (b + 1) * LANES]
        chosen = part[:taps]
        for g in range(1, filters_here):
            chosen = jnp.where(lanes == g, part[g * taps : (g + 1) * taps], chosen)
        results.append(chosen)
    return jnp.concatenate(results, 0)


def back_kernel(grad_ref, after_ref, key_ref, value_ref, toep_ref, skip_ref, gk_ref, gv_ref):
    taps = toep_ref.shape[1] // 2
    grad = grad_ref[...]
    joined = jnp.concatenate([grad, after_ref[...]], 0)
    windows = [joined[b * taps : (b + 2) * taps] for b in range(grad.shape[0] // taps)]
    grad_mixed = conv_blocks(toep_ref[...], windows) + skip_ref[...] * grad.astype(jnp.float32)
    gk_ref[...] = (grad_mixed * value_ref[...].astype(jnp.float32)).astype(jnp.bfloat16)
    gv_ref[...] = (grad_mixed * key_ref[...].astype(jnp.float32)).astype(jnp.bfloat16)


def tile_call(kernel, operands, out_types, groups, name):
    rows, channels = operands[0].shape
    tiles = channels // LANES

    def spec(array):
        if array.shape[0] % groups == 0 and array.shape[1] != channels:
            return pl.BlockSpec((array.shape[0] // tiles, array.shape[1]), lambda i: (i, 0))
        return pl.BlockSpec((array.shape[0], LANES), lambda i: (0, i))

    return pl.pallas_call(
        kernel,
        grid=(tiles,),
        in_specs=[spec(a) for a in operands],
        out_specs=[pl.BlockSpec((rows, LANES), lambda i: (0, i)) for _ in out_types],
        out_shape=[jax.ShapeDtypeStruct((rows, channels), t) for t in out_types],
        compiler_params=pltpu.CompilerParams(vmem_limit_bytes=VMEM_LIMIT),
        cost_estimate=pl.CostEstimate(
            flops=rows * channels * 4096, bytes_accessed=rows * channels * 12, transcendentals=0
        ),
        name=name,
    )(*operands)


def product_kernel(
    weight_ref, cot_ref, input_ref, gated_ref, query_ref, back_up_ref, down_ref, proj_ref, up_ref,
    out_ref, gq_ref, gg_ref, total,
):
    step = pl.program_id(0)
    parts, _, width = weight_ref.shape

    @pl.when(step == 0)
    def _():
        total[...] = adapter_scale * jnp.dot(
            proj_ref[...], up_ref[...], preferred_element_type=jnp.float32
        )

    nt = (((1,), (1,)), ((), ()))
    back = adapter_scale * lax.dot_general(
        back_up_ref[...], down_ref[...], nt, preferred_element_type=jnp.float32
    )
    for f in range(parts):
        columns = slice(f * width, (f + 1) * width)
        weight = weight_ref[f]
        back = back + lax.dot_general(
            cot_ref[:, columns], weight, nt, preferred_element_type=jnp.float32
        )
        total[:, columns] += jnp.dot(input_ref[...], weight, preferred_element_type=jnp.float32)
    gq_ref[...] = (back * gated_ref[...]).astype(jnp.bfloat16)
    gg_ref[...] = (back * query_ref[...].astype(jnp.float32)).astype(jnp.bfloat16)

    @pl.when(step == pl.num_programs(0) - 1)
    def _():
        out_ref[...] = total[...].astype(jnp.bfloat16)


def products(weight, cot, gated_input, gated, query, back_up, down, proj, up):
    parts, channels, width = weight.shape
    rows = cot.shape[0]
    features = parts * width
    rank = down.shape[1]
    block = 512
    whole = lambda i: (0, 0)
    tile = pl.BlockSpec((rows, block), lambda i: (0, i))
    return pl.pallas_call(
        product_kernel,
        grid=(channels // block,),
        in_specs=[
            pl.BlockSpec((parts, block, width), lambda i: (0, i, 0)),
            pl.BlockSpec((rows, features), whole),
            tile,
            tile,
            tile,
            pl.BlockSpec((rows, rank), whole),
            pl.BlockSpec((block, rank), lambda i: (i, 0)),
            pl.BlockSpec((rows, rank), whole),
            pl.BlockSpec((rank, features), whole),
        ],
        out_specs=[pl.BlockSpec((rows, features), whole), tile, tile],
        out_shape=[
            jax.ShapeDtypeStruct((rows, features), jnp.bfloat16),
            jax.ShapeDtypeStruct((rows, channels), jnp.bfloat16),
            jax.ShapeDtypeStruct((rows, channels), jnp.bfloat16),
        ],
        scratch_shapes=[pltpu.VMEM((rows, features), jnp.float32)],
        compiler_params=pltpu.CompilerParams(vmem_limit_bytes=VMEM_LIMIT),
        cost_estimate=pl.CostEstimate(
            flops=4 * rows * channels * features,
            bytes_accessed=2 * channels * features,
            transcendentals=0,
        ),
        name="products",
    )(weight, cot, gated_input, gated, query, back_up, down, proj, up)


def local(
    query_branch,
    key_branch,
    value_branch,
    cotangent,
    quantized_weight_codes,
    scale_code_bytes,
    row_scale_second,
    filters,
    channel_skip_weight,
    adapter_down_weight,
    adapter_up_weight,
):
    groups, filter_len = filters.shape
    query, key, value, cot = query_branch[0], key_branch[0], value_branch[0], cotangent[0]
    row_count = query.shape[0]
    n_f, n_c = lax.axis_size("fsdp"), lax.axis_size("ctx")
    token_count = query_branch.shape[0] * row_count * n_c * n_f
    multiplier = adapter_scale / math.sqrt(token_count)
    skip = channel_skip_weight[None]

    tail = row_count - filter_len
    mixed_tail = (
        key[tail:].astype(jnp.float32) * value[tail:].astype(jnp.float32)
    ).astype(jnp.bfloat16)
    piece = dequantize(quantized_weight_codes, scale_code_bytes, row_scale_second)
    taps = filters.astype(jnp.float32)
    zeros = jnp.zeros((groups, filter_len), jnp.float32)
    back_base = jnp.concatenate([taps, zeros], 1)
    ahead_base = jnp.concatenate([zeros[:, :1], jnp.flip(taps, 1), zeros[:, 1:]], 1)

    weight, gated, gated_input, grad_down, grad_up, proj, back_up, down, up, toep = gather_weight(
        mixed_tail, piece, adapter_down_weight, adapter_up_weight, cot, query, key, value,
        ahead_base, skip, back_base, n_f, n_c, multiplier,
    )
    output, grad_query, grad_gated = products(
        weight, cot, gated_input, gated, query, back_up, down, proj, up
    )
    after = from_behind(grad_gated[:filter_len], "ctx", -1)
    grad_key, grad_value = tile_call(
        back_kernel,
        (grad_gated, after, key, value, toep, skip),
        (jnp.bfloat16, jnp.bfloat16),
        groups,
        "conv_back",
    )
    return (
        output[None],
        grad_query[None],
        grad_key[None],
        grad_value[None],
        grad_down,
        grad_up,
    )


def solution(mesh):
    return jax.shard_map(
        local,
        mesh=mesh,
        in_specs=(
            P("fsdp", "ctx", None),
            P("fsdp", "ctx", None),
            P("fsdp", "ctx", None),
            P("fsdp", "ctx", None),
            P("ctx", "fsdp"),
            P("ctx", "fsdp"),
            P("ctx"),
            P(),
            P(),
            P("ctx", None),
            P(None, "fsdp"),
        ),
        out_specs=(
            P("fsdp", "ctx", None),
            P("fsdp", "ctx", None),
            P("fsdp", "ctx", None),
            P("fsdp", "ctx", None),
            P("ctx", None),
            P(None, "fsdp"),
        ),
        check_vma=False,
    )
```
